32 devices in a mesh: scen: 16 (over z, y, x), sub: 2 (over core).
Axes of the slice: x: 2, y: 2, z: 4, core: 2. Of those that a mesh axis runs over, the one named last changes fastest.
Arguments:
- disturbance: float32 [8, 32, 48, 2048], P('sub', None, None, 'scen'), may hold values from -6 to 6
- prior_states: float32 [8, 32, 48, 2048], P('sub', None, None, 'scen'), may hold values from -6 to 6
- initial_state: float32 [8, 48], P('sub'), may hold values from -6 to 6
- scaled_duals: float32 [8, 7, 16, 2048], P('sub', None, None, 'scen'), may hold values from -3 to 3
- dynamics: float32 [8, 48, 48], P('sub'), may hold values from -0.5 to 0.5
- actuation: float32 [8, 48, 16], P('sub'), may hold values from -0.4375 to 0.4375
- cost_to_go: float32 [8, 32, 48, 48], P('sub'), may hold values from -0.875 to 0.875
- inverses: float32 [8, 32, 16, 16], P('sub'), may hold values from -0.75 to 0.75
- couplers: float32 [8, 2, 48, 48], replicated, may hold values from -0.625 to 0.625
- neighbours: int32 [8, 2], replicated, may hold values from 0 to 7, as said below
- branches: int32 [6, 2048], P(None, 'scen'), may hold values from 0 to 1, as said below
Outputs:
- states: float32 [8, 32, 48, 2048], P('sub', None, None, 'scen')
- controls: float32 [8, 32, 16, 2048], P('sub', None, None, 'scen')
- new_duals: float32 [8, 7, 16, 2048], P('sub', None, None, 'scen')
The draws below stay inside these ranges and needn't reach their ends.
Inputs may be any that keep to these rules, and one draw needn't show every extreme that they name: For every t from 0 to 6, the scenarios that agree on branches 0 to t - 1 number exactly 2048 / 2^t. `neighbours`: each row names 2 different subsystems, none of them the row's own.
All inputs are finite; a program needn't handle non-finite values.
Results may differ from the reference program's by a relative error of at most 0.0001.
Values sent between devices are 32-bit elements; how exact they have to be, the bound alone decides.
A program may use at most 128 MiB of HBM per device.

```python
import jax
import jax.numpy as jnp
from jax import lax

NX = 48
NU = 16
NCP = 48
NB = 2
H = 32
ROBUST = 7
SWEEPS = 2
SCEN = 2048
SUBS = 8


def draw_neighbours(key, part):
    scores = jax.random.randint(jax.random.fold_in(key, 11), (SUBS, SUBS - 1), 0, 1 << 20)
    scores = scores * SUBS + jnp.arange(SUBS - 1, dtype=jnp.int32)[None, :]
    ranking = jnp.argsort(scores, axis=1)
    offsets = ranking[:, :NB].astype(jnp.int32) + 1
    return ((jnp.arange(SUBS, dtype=jnp.int32)[:, None] + offsets) % SUBS).astype(jnp.int32)


def draw_branches(key, part):
    shuffled = jax.random.permutation(jax.random.fold_in(key, 12), SCEN).astype(jnp.int32)
    powers = (2 ** jnp.arange(ROBUST - 1)).astype(jnp.int32)
    return (shuffled[None, :] // powers[:, None] % 2).astype(jnp.int32)


def steps_of(rng, shape, shards, least, largest):
    factor_of = 1.0
    for axis_at, blocks in shards:
        draws = jax.random.uniform(jax.random.fold_in(jax.random.fold_in(rng, 6), axis_at), (blocks,), jnp.float32, least / len(shards), largest / len(shards))
        factor_of = factor_of * jnp.repeat(jnp.exp(draws), shape[axis_at] // blocks).reshape((-1,) + (1,) * (len(shape) - 1 - axis_at))
    return factor_of


def noise(key, extent, spread, bound, cuts=(), kind=jnp.bfloat16):
    values = jax.random.normal(key, extent, jnp.float32) * spread
    if len(cuts) > 0:
        values = steps_of(key, extent, cuts, -0.22, 0.18) * values
    return jnp.clip(values, min=-bound, max=bound).astype(kind)


def setup_inputs(seed: int = 0) -> dict:
    arg_keys = jax.random.split(jax.random.key(seed), 12)
    return {
        "disturbance": noise(arg_keys[0], (SUBS, H, NX, SCEN), 1.0, 6.0, ((0, 2), (3, 16)), jnp.float32),
        "prior_states": noise(arg_keys[1], (SUBS, H, NCP, SCEN), 1.0, 6.0, ((0, 2), (3, 16)), jnp.float32),
        "initial_state": noise(arg_keys[2], (SUBS, NX), 1.0, 6.0, ((0, 2),), jnp.float32),
        "scaled_duals": noise(arg_keys[3], (SUBS, ROBUST, NU, SCEN), 0.5, 3.0, ((0, 2), (3, 16)), jnp.float32),
        "dynamics": noise(arg_keys[4], (SUBS, NX, NX), (3 * NX) ** -0.5, 0.5, ((0, 2),), jnp.float32),
        "actuation": noise(arg_keys[5], (SUBS, NX, NU), (4 * NX) ** -0.5, 0.4375, ((0, 2),), jnp.float32),
        "cost_to_go": noise(arg_keys[6], (SUBS, H, NX, NX), NX ** -0.5, 0.875, ((0, 2),), jnp.float32),
        "inverses": noise(arg_keys[7], (SUBS, H, NU, NU), (4 * NU) ** -0.5, 0.75, ((0, 2),), jnp.float32),
        "couplers": noise(arg_keys[8], (SUBS, NB, NX, NCP), (NB * NCP) ** -0.5, 0.625, (), jnp.float32),
        "neighbours": draw_neighbours(jax.random.fold_in(arg_keys[11], 71), 0),
        "branches": draw_branches(jax.random.fold_in(arg_keys[11], 71), 0),
    }


penalty = 1.0
highest = lax.Precision.HIGHEST


def time_first(values):
    return jnp.moveaxis(values, 1, 0)


def feedback(dynamics, actuation, cost_to_go, inverses):
    shaped = jnp.einsum('mau,mtab->mtub', actuation, cost_to_go, precision=highest)
    shaped = jnp.einsum('mtub,mbc->mtuc', shaped, dynamics, precision=highest)
    return -jnp.einsum('mtuv,mtvc->mtuc', inverses, shaped, precision=highest)


def node_table(branches):
    robust = branches.shape[0] + 1
    powers = (2 ** jnp.arange(robust - 1)).astype(jnp.int32)
    climbed = jnp.cumsum(branches * powers[:, None], axis=0).astype(jnp.int32)
    node_ids = jnp.concatenate([jnp.zeros((1, branches.shape[1]), jnp.int32), climbed], axis=0)
    labels = jnp.arange(2 ** (robust - 1), dtype=jnp.int32)
    return (node_ids[:, :, None] == labels[None, None, :]).astype(jnp.float32)


def riccati(dynamics, actuation, cost_to_go, inverses, feedbacks, initial_state, drive_terms, linear):
    def backward(costate, pieces):
        weight, inverse, gain_now, drive_now, linear_now = pieces
        grown_sum = jnp.einsum('mab,mbs->mas', weight, drive_now, precision=highest) + costate
        gradient = linear_now + jnp.einsum('mau,mas->mus', actuation, grown_sum, precision=highest)
        offset = -jnp.einsum('muv,mvs->mus', inverse, gradient, precision=highest)
        costate = (jnp.einsum('mba,mbs->mas', dynamics, grown_sum, precision=highest)
                   + jnp.einsum('mua,mus->mas', gain_now, gradient, precision=highest))
        return costate, offset

    zero_state = jnp.zeros(drive_terms[:, 0].shape, jnp.float32)
    final_costate, offsets = lax.scan(
        backward, zero_state,
        (time_first(cost_to_go), time_first(inverses), time_first(feedbacks), time_first(drive_terms), time_first(linear)),
        reverse=True, unroll=4)

    def forward(state_now, pieces):
        gain_now, offset, drive_now = pieces
        control = jnp.einsum('mua,mas->mus', gain_now, state_now, precision=highest) + offset
        state_now = (jnp.einsum('mab,mbs->mas', dynamics, state_now, precision=highest)
                     + jnp.einsum('mau,mus->mas', actuation, control, precision=highest) + drive_now)
        return state_now, (state_now, control)

    begin_state = jnp.broadcast_to(initial_state[:, :, None], drive_terms[:, 0].shape).astype(jnp.float32)
    last_state, outputs = lax.scan(forward, begin_state, (time_first(feedbacks), offsets, time_first(drive_terms)), unroll=4)
    return jnp.moveaxis(outputs[0], 0, 1), jnp.moveaxis(outputs[1], 0, 1)


def reference(disturbance, prior_states, initial_state, scaled_duals, dynamics, actuation, cost_to_go, inverses, couplers, neighbours, branches):
    feedbacks = feedback(dynamics, actuation, cost_to_go, inverses)
    node_onehot = node_table(branches)
    robust = scaled_duals.shape[1]
    counts = disturbance.shape[3] / (2.0 ** jnp.arange(robust))
    duals = scaled_duals
    consensus = jnp.zeros_like(duals)
    previous = prior_states
    zero_tail = jnp.zeros((duals.shape[0], disturbance.shape[1] - robust) + duals.shape[2:], jnp.float32)
    for sweep_index in range(SWEEPS):
        picked = previous[neighbours]
        drive_terms = disturbance + jnp.einsum('ieab,ietbs->itas', couplers, picked, precision=highest)
        linear = jnp.concatenate([penalty * (duals - consensus), zero_tail], axis=1)
        states, controls = riccati(dynamics, actuation, cost_to_go, inverses, feedbacks, initial_state, drive_terms, linear)
        averaged_in = controls[:, :robust] + duals
        totals = jnp.einsum('mtus,tsn->tmun', averaged_in, node_onehot, precision=highest)
        node_means = totals / counts[:, None, None, None]
        consensus = jnp.einsum('tmun,tsn->mtus', node_means, node_onehot, precision=highest)
        duals = duals + controls[:, :robust] - consensus
        previous = states[:, :, :prior_states.shape[2]]
    return states, controls, duals
```

```python
import functools

import jax
import jax.numpy as jnp
from jax import lax
from jax.experimental import pallas as pl
from jax.experimental.pallas import tpu as pltpu
from jax.sharding import PartitionSpec as P

SWEEPS = 2
F32, BF16 = jnp.float32, jnp.bfloat16
VMEM_BYTES = 56 * 1024 * 1024


def exact_dot(a, b):
    return jnp.dot(a, b, precision=lax.Precision.HIGHEST, preferred_element_type=F32)


def halves(x):
    hi = x.astype(BF16)
    return hi, (x - hi.astype(F32)).astype(BF16)


def wide(w):
    hi, lo = halves(w)
    return jnp.concatenate([hi.astype(F32), lo.astype(F32), hi.astype(F32)], axis=1).astype(BF16)


def tall(x):
    hi, lo = halves(x)
    return jnp.concatenate([hi, hi, lo], axis=0)


def mxu(a, b):
    return jnp.dot(a, b, preferred_element_type=F32)


def prepare(t, dyn, act, ctg, inv, wb, wf, wp, dyn_t, act_t):
    subs = dyn.shape[0]
    for m in range(subs):
        a, b, at, bt = dyn[m], act[m], dyn_t[m], act_t[m]
        p, g = ctg[m, t], inv[m, t]
        gain = -exact_dot(g, exact_dot(exact_dot(bt, p), a))
        closed = a + exact_dot(b, gain)
        back = -exact_dot(g, bt)
        bg = -exact_dot(b, g)
        left = jnp.concatenate([closed.T, back, exact_dot(b, back)], axis=0)
        right = jnp.concatenate([gain.T, -g, bg], axis=0)
        wb[m, t] = jnp.concatenate([wide(left).astype(F32), wide(right).astype(F32)], axis=1).astype(BF16)
        wf[m, t] = wide(jnp.concatenate([closed, gain], axis=0))
        wp[m, t] = wide(p)


def couple(own_first, other_first, neigh, coup, cx):
    subs, nb, nx, ncp = coup.shape
    for side, first in enumerate((own_first, other_first)):
        for i in range(subs):
            for j in range(subs):
                total = jnp.zeros((nx, ncp), F32)
                for e in range(nb):
                    hit = neigh[i, e] == first + j
                    total = total + jnp.where(hit, coup[i, e], 0.0)
                hi, lo = halves(total)
                at = (side * subs + j) * ncp
                cx[0, i * nx:(i + 1) * nx, at:at + ncp] = hi
                cx[1, i * nx:(i + 1) * nx, at:at + ncp] = lo


def influence(t, own, other, cx):
    subs = own.shape[0]
    blocks = [own[j, t] for j in range(subs)] + [other[j, t] for j in range(subs)]
    x = jnp.concatenate(blocks, axis=0)
    hi, lo = halves(x)
    return mxu(cx[0], hi) + mxu(cx[1], hi) + mxu(cx[0], lo)


def sweep(own, other, dist, linear, init, wb, wf, wp, cx, drive, offs, states, controls):
    subs, steps, nx, s = dist.shape
    nu = controls.shape[2]
    robust = linear.shape[1]

    def grow(t):
        flow = influence(t, own, other, cx)
        out = []
        for i in range(subs):
            d = dist[i, t] + flow[i * nx:(i + 1) * nx]
            drive[i, t] = d
            out.append(mxu(wp[i, t], tall(d)))
        return tuple(out)

    def back(t, carry, with_linear):
        costate, q = carry
        ahead = grow(jnp.maximum(t - 1, 0))
        after = []
        for i in range(subs):
            right = tall(q[i] + costate[i])
            if with_linear:
                right = jnp.concatenate([right, tall(linear[i, t])], axis=0)
                y = mxu(wb[i, t], right)
            else:
                y = mxu(wb[i, t, :, :3 * nx], right)
            offs[i, t] = y[nx:nx + nu]
            states[i, t] = y[nx + nu:]
            after.append(y[:nx])
        return tuple(after), ahead

    zero = tuple(jnp.zeros((nx, s), F32) for _ in range(subs))
    carry = (zero, grow(steps - 1))
    carry = lax.fori_loop(0, steps - robust, lambda k, c: back(steps - 1 - k, c, False), carry)
    carry = lax.fori_loop(0, robust, lambda k, c: back(robust - 1 - k, c, True), carry)

    def ahead(t, x):
        after = []
        for i in range(subs):
            y = mxu(wf[i, t], tall(x[i]))
            controls[i, t] = y[nx:] + offs[i, t]
            now = y[:nx] + (states[i, t] + drive[i, t])
            states[i, t] = now
            after.append(now)
        return tuple(after)

    x = tuple(jnp.broadcast_to(init[i], (nx, s)) for i in range(subs))
    return ahead, x


def member(t, ids, lanes):
    s = ids.shape[1]
    place = lax.broadcasted_iota(jnp.int32, (lanes, s), 0)
    return jnp.where(place == ids[t:t + 1, :] + (2**t - 1), 1.0, 0.0).astype(BF16)


def node_sums(averaged, ids, lanes):
    robust = len(averaged)
    total = None
    for t in range(robust):
        hot = member(t, ids, lanes)
        for part in halves(averaged[t]):
            term = lax.dot_general(part, hot, (((1,), (1,)), ((), ())), preferred_element_type=F32)
            total = term if total is None else total + term
    return total


def node_means(totals, robust, scen_total):
    place = lax.broadcasted_iota(jnp.int32, totals.shape, 1)
    shares = jnp.ones(totals.shape, F32)
    for t in range(1, robust):
        shares = jnp.where(place >= 2**t - 1, float(2**t), shares)
    return totals * (shares / float(scen_total))


def spread(means, t, ids):
    hot = member(t, ids, means.shape[1])
    hi, lo = halves(means)
    return mxu(hi, hot) + mxu(lo, hot)


def gathered(controls, duals, t):
    subs = duals.shape[0]
    return jnp.concatenate([controls[i, t] + duals[i, t] for i in range(subs)], axis=0)


def first_kernel(firsts, neigh, own, other, dist, duals, init, dyn, act, ctg, inv, coup, ids,
                 states, controls, sums, wb, wf, wp, cx, drive, offs, dyn_t, act_t):
    subs, robust = duals.shape[:2]
    steps = dist.shape[1]
    for m in range(subs):
        dyn_t[m] = dyn[m].T
        act_t[m] = act[m].T
    couple(firsts[0], firsts[1], neigh, coup, cx)

    def prep(t, c):
        prepare(t, dyn, act, ctg, inv, wb, wf, wp, dyn_t, act_t)
        return c

    lax.fori_loop(0, steps, prep, 0)
    step, x = sweep(own, other, dist, duals, init, wb, wf, wp, cx, drive, offs, states, controls)
    lax.fori_loop(0, steps, step, x)
    ids_now = ids[...]
    averaged = [gathered(controls, duals, t) for t in range(robust)]
    sums[...] = node_sums(averaged, ids_now, sums.shape[1])


def second_kernel(scen_total, own, other, dist, duals, init, before, ids, totals, wb, wf, wp, cx,
                  states, controls, sums, averaged_out, drive, offs, linear, duals_now):
    subs, robust, nu, s = duals.shape
    steps = dist.shape[1]
    ids_now = ids[...]
    means = node_means(totals[...], robust, scen_total)
    for t in range(robust):
        consensus = spread(means, t, ids_now)
        for i in range(subs):
            c = consensus[i * nu:(i + 1) * nu]
            now = duals[i, t] + before[i, t] - c
            duals_now[i, t] = now
            linear[i, t] = now - c
    step, x = sweep(own, other, dist, linear, init, wb, wf, wp, cx, drive, offs, states, controls)
    lax.fori_loop(0, steps, step, x)
    averaged = []
    for t in range(robust):
        v = gathered(controls, duals_now, t)
        averaged.append(v)
        for i in range(subs):
            averaged_out[i, t] = v[i * nu:(i + 1) * nu]
    sums[...] = node_sums(averaged, ids_now, sums.shape[1])


def last_kernel(scen_total, averaged, ids, totals, out):
    subs, robust, nu, s = averaged.shape
    means = node_means(totals[...], robust, scen_total)
    for t in range(robust):
        consensus = spread(means, t, ids[...])
        for i in range(subs):
            out[i, t] = averaged[i, t] - consensus[i * nu:(i + 1) * nu]


def shards(mesh, disturbance, prior_states, initial_state, scaled_duals, dynamics, actuation, cost_to_go,
           inverses, couplers, neighbours, branches):
    subs, steps, nx, s = disturbance.shape
    robust, nu = scaled_duals.shape[1:3]
    ncp = prior_states.shape[2]
    n_scen, n_sub = mesh.shape["scen"], mesh.shape["sub"]
    scen_total = s * n_scen
    me = lax.axis_index("sub")
    first = me * subs
    other_first = ((me + 1) % n_sub) * subs
    swap = [((k + 1) % n_sub, k) for k in range(n_sub)]
    coup = lax.dynamic_slice_in_dim(couplers, first, subs, 0)
    neigh = lax.dynamic_slice_in_dim(neighbours, first, subs, 0)
    firsts = jnp.stack([first, other_first]).astype(jnp.int32)
    rows = [jnp.zeros((s,), jnp.int32)]
    for k in range(branches.shape[0]):
        rows.append(rows[-1] + branches[k] * 2**k)
    ids = jnp.stack(rows)
    lanes = 2**robust
    init = initial_state[:, :, None]

    vm, sm = pl.BlockSpec(memory_space=pltpu.VMEM), pl.BlockSpec(memory_space=pltpu.SMEM)
    big = jax.ShapeDtypeStruct((subs, steps, nx, s), F32)
    small = jax.ShapeDtypeStruct((subs, steps, nu, s), F32)
    sums = jax.ShapeDtypeStruct((subs * nu, lanes), F32)
    few = jax.ShapeDtypeStruct((subs, robust, nu, s), F32)
    weights = [
        jax.ShapeDtypeStruct((subs, steps, 2 * nx + nu, 3 * (nx + nu)), BF16),
        jax.ShapeDtypeStruct((subs, steps, nx + nu, 3 * nx), BF16),
        jax.ShapeDtypeStruct((subs, steps, nx, 3 * nx), BF16),
        jax.ShapeDtypeStruct((2, subs * nx, 2 * subs * ncp), BF16),
    ]
    params = pltpu.CompilerParams(vmem_limit_bytes=VMEM_BYTES)
    scratch = [pltpu.VMEM((subs, steps, nx, s), F32), pltpu.VMEM((subs, steps, nu, s), F32)]
    other = lax.ppermute(prior_states, "sub", swap)
    states, controls, partial, *made = pl.pallas_call(
        first_kernel,
        out_shape=[big, small, sums] + weights,
        in_specs=[sm, sm] + [vm] * 11,
        out_specs=[vm] * 7,
        scratch_shapes=scratch + [pltpu.VMEM((subs, nx, nx), F32), pltpu.VMEM((subs, nu, nx), F32)],
        compiler_params=params,
    )(firsts, neigh, prior_states, other, disturbance, scaled_duals, init, dynamics, actuation,
      cost_to_go, inverses, coup, ids)
    other = lax.ppermute(states[:, :, :ncp], "sub", swap)
    totals = lax.psum(partial, "scen")
    states, controls, partial, averaged = pl.pallas_call(
        functools.partial(second_kernel, scen_total),
        out_shape=[big, small, sums, few],
        in_specs=[vm] * 12,
        out_specs=[vm] * 4,
        scratch_shapes=scratch + [pltpu.VMEM(few.shape, F32), pltpu.VMEM(few.shape, F32)],
        compiler_params=params,
    )(states, other, disturbance, scaled_duals, init, controls[:, :robust], ids, totals, *made)
    totals = lax.psum(partial, "scen")
    new_duals = pl.pallas_call(
        functools.partial(last_kernel, scen_total),
        out_shape=few,
        in_specs=[vm] * 3,
        out_specs=vm,
        compiler_params=params,
    )(averaged, ids, totals)
    return states, controls, new_duals


def solution(mesh):
    wide_spec = P("sub", None, None, "scen")
    placed = (wide_spec, wide_spec, P("sub", None), wide_spec, P("sub", None, None), P("sub", None, None),
              P("sub", None, None, None), P("sub", None, None, None), P(), P(), P(None, "scen"))
    return jax.shard_map(
        functools.partial(shards, mesh), mesh=mesh, in_specs=placed, out_specs=(wide_spec,) * 3,
        check_vma=False,
    )
```

```python
import functools

import jax
import jax.numpy as jnp
from jax import lax
from jax.experimental import pallas as pl
from jax.experimental.pallas import tpu as pltpu
from jax.sharding import PartitionSpec as P

SWEEPS = 2
F32, BF16 = jnp.float32, jnp.bfloat16
VMEM_BYTES = 56 * 1024 * 1024


def halves(x):
    hi = x.astype(BF16)
    return hi, (x - hi.astype(F32)).astype(BF16)


def wide(w):
    hi, lo = halves(w)
    return jnp.concatenate([hi.astype(F32), lo.astype(F32), hi.astype(F32)], axis=1).astype(BF16)


def tall(x):
    hi, lo = halves(x)
    return jnp.concatenate([hi, hi, lo], axis=0)


def mxu(a, b):
    return jnp.dot(a, b, preferred_element_type=F32)


def dot3(a, b):
    a_hi, a_lo = halves(a)
    b_hi, b_lo = halves(b)
    return mxu(a_hi, b_hi) + (mxu(a_lo, b_hi) + mxu(a_hi, b_lo))


def prepare(times, dyn, act_t, ctg, inv, wb, wf, wp):
    subs, nx = dyn.shape[:2]
    nu = act_t.shape[1]
    work = [(m, t) for t in times for m in range(subs)]
    bt = [act_t[m] for m in range(subs)]
    at = [tall(dyn[m]) for m in range(subs)]
    pa = []
    for m, t in work:
        p = wide(ctg[m, t])
        wp[m, t] = p
        pa.append(mxu(p, at[m]))
    g = [inv[m, t] for m, t in work]
    bg = [dot3(bt[m].T, g[k]) for k, (m, t) in enumerate(work)]
    x2 = [dot3(bt[m], pa[k]) for k, (m, t) in enumerate(work)]
    both = [-jnp.concatenate([g[k], bg[k]], axis=0) for k in range(len(work))]
    low = [dot3(both[k], bt[m]) for k, (m, t) in enumerate(work)]
    gain = [dot3(both[k], x2[k]) for k in range(len(work))]
    for k, (m, t) in enumerate(work):
        front = jnp.concatenate([dyn[m] + gain[k][nu:], gain[k][:nu]], axis=0)
        wf[m, t] = wide(front)
        bottom = jnp.concatenate([low[k], both[k]], axis=1)
        wb[m, t] = wide(jnp.concatenate([front.T, bottom], axis=0))


def couple(subs, own_first, other_first, neigh, coup, cx):
    nb, nx, ncp = coup.shape[1:]
    for side, first in enumerate((own_first, other_first)):
        for i in range(subs):
            for j in range(subs):
                total = jnp.zeros((nx, ncp), F32)
                for e in range(nb):
                    hit = neigh[e, own_first + i] == first + j
                    total = total + jnp.where(hit, coup[own_first + i, e], 0.0)
                hi, lo = halves(total)
                at = (side * subs + j) * ncp
                cx[0, i * nx:(i + 1) * nx, at:at + ncp] = hi
                cx[1, i * nx:(i + 1) * nx, at:at + ncp] = lo


def influence(t, own, other, cx):
    subs = own.shape[0]
    blocks = [own[j, t] for j in range(subs)] + [other[j, t] for j in range(subs)]
    x = jnp.concatenate(blocks, axis=0)
    hi, lo = halves(x)
    return mxu(cx[0], hi) + mxu(cx[1], hi) + mxu(cx[0], lo)


def sweep(own, other, dist, linear, init, wb, wf, wp, cx, drive, offs, states, controls):
    subs, steps, nx, s = dist.shape
    nu = controls.shape[2]
    robust = linear.shape[1]

    def grow(t):
        flow = influence(t, own, other, cx)
        out = []
        for i in range(subs):
            d = dist[i, t] + flow[i * nx:(i + 1) * nx]
            drive[i, t] = d
            out.append(mxu(wp[i, t], tall(d)))
        return tuple(out)

    def back(t, carry, with_linear):
        costate, q = carry
        ahead = grow(jnp.maximum(t - 1, 0))
        after = []
        for i in range(subs):
            push = linear[i, t] if with_linear else jnp.zeros((nu, s), F32)
            y = mxu(wb[i, t], tall(jnp.concatenate([q[i] + costate[i], push], axis=0)))
            offs[i, t] = y[nx:nx + nu]
            states[i, t] = y[nx + nu:]
            after.append(y[:nx])
        return tuple(after), ahead

    zero = tuple(jnp.zeros((nx, s), F32) for _ in range(subs))
    carry = (zero, grow(steps - 1))
    carry = lax.fori_loop(0, steps - robust, lambda k, c: back(steps - 1 - k, c, False), carry)
    carry = lax.fori_loop(0, robust, lambda k, c: back(robust - 1 - k, c, True), carry)

    def ahead(t, x):
        after = []
        for i in range(subs):
            y = mxu(wf[i, t], tall(x[i]))
            controls[i, t] = y[nx:] + offs[i, t]
            now = y[:nx] + (states[i, t] + drive[i, t])
            states[i, t] = now
            after.append(now)
        return tuple(after)

    x = tuple(jnp.broadcast_to(init[...].T[:, i:i + 1], (nx, s)) for i in range(subs))
    return ahead, x


def member(t, ids, lanes):
    s = ids.shape[1]
    place = lax.broadcasted_iota(jnp.int32, (lanes, s), 0)
    return jnp.where(place == ids[t:t + 1, :] + (2**t - 1), 1.0, 0.0).astype(BF16)


def node_ids(branches):
    rows = [jnp.zeros((1, branches.shape[1]), jnp.int32)]
    for k in range(branches.shape[0]):
        rows.append(rows[-1] + branches[k:k + 1] * 2**k)
    return jnp.concatenate(rows, axis=0)


def put(sums, values):
    count, rows, lanes = sums.shape
    extra = count * rows - values.shape[0]
    if extra:
        values = jnp.concatenate([values, jnp.zeros((extra, lanes), F32)], axis=0)
    for k in range(count):
        sums[k] = values[k * rows:(k + 1) * rows]


def take(totals, rows):
    return jnp.concatenate([totals[k] for k in range(-(-rows // totals.shape[1]))], axis=0)[:rows]


def reduce_kernel(part, out, land, full, send_a, recv_a, send_b, recv_b):
    n = part.shape[0]
    me = lax.axis_index("scen")
    barrier = pltpu.get_barrier_semaphore()

    def over(step):
        def body(k, c):
            step(k, lax.rem(me + k, n))
            return c

        lax.fori_loop(1, n, body, 0)

    def piece(k, to):
        return pltpu.make_async_remote_copy(
            src_ref=part.at[to], dst_ref=land.at[k], send_sem=send_a.at[k], recv_sem=recv_a.at[k],
            device_id={"scen": to}, device_id_type=pl.DeviceIdType.MESH)

    def whole(k, to):
        return pltpu.make_async_remote_copy(
            src_ref=full.at[me], dst_ref=full.at[me], send_sem=send_b.at[k], recv_sem=recv_b.at[k],
            device_id={"scen": to}, device_id_type=pl.DeviceIdType.MESH)

    over(lambda k, to: pl.semaphore_signal(
        barrier, inc=1, device_id={"scen": to}, device_id_type=pl.DeviceIdType.MESH))
    pl.semaphore_wait(barrier, n - 1)
    over(lambda k, to: piece(k, to).start())
    over(lambda k, to: piece(k, to).wait_recv())
    full[me] = lax.fori_loop(1, n, lambda k, c: c + land[k], part[me])
    over(lambda k, to: whole(k, to).start())
    over(lambda k, to: piece(k, to).wait_send())
    over(lambda k, to: whole(k, to).wait_recv())
    over(lambda k, to: whole(k, to).wait_send())
    out[...] = full[...]


def all_sum(part):
    n = part.shape[0]
    vm = pl.BlockSpec(memory_space=pltpu.VMEM)
    return pl.pallas_call(
        reduce_kernel,
        out_shape=jax.ShapeDtypeStruct(part.shape, F32),
        in_specs=[vm],
        out_specs=vm,
        scratch_shapes=[pltpu.VMEM(part.shape, F32)] * 2 + [pltpu.SemaphoreType.DMA((n,))] * 4,
        compiler_params=pltpu.CompilerParams(collective_id=0, has_side_effects=True),
    )(part)


def node_sums(averaged, ids, lanes):
    robust = len(averaged)
    total = None
    for t in range(robust):
        hot = member(t, ids, lanes)
        for part in halves(averaged[t]):
            term = lax.dot_general(part, hot, (((1,), (1,)), ((), ())), preferred_element_type=F32)
            total = term if total is None else total + term
    return total


def node_means(totals, robust, scen_total):
    place = lax.broadcasted_iota(jnp.int32, totals.shape, 1)
    shares = jnp.ones(totals.shape, F32)
    for t in range(1, robust):
        shares = jnp.where(place >= 2**t - 1, float(2**t), shares)
    return totals * (shares / float(scen_total))


def spread(means, t, ids):
    hot = member(t, ids, means.shape[1])
    hi, lo = halves(means)
    return mxu(hi, hot) + mxu(lo, hot)


def gathered(controls, duals, t):
    subs = duals.shape[0]
    return jnp.concatenate([controls[i, t] + duals[i, t] for i in range(subs)], axis=0)


def first_kernel(neigh, own, other, dist, duals, init, dyn, act_t, ctg, inv, coup, branches,
                 states, controls, sums, wb, wf, wp, cx, drive, offs):
    subs, robust = duals.shape[:2]
    steps = dist.shape[1]
    n_sub = coup.shape[0] // subs
    me = lax.axis_index("sub")
    couple(subs, me * subs, lax.rem(me + 1, n_sub) * subs, neigh, coup, cx)
    each = 2 if steps % 2 == 0 else 1

    def prep(k, c):
        prepare([k * each + r for r in range(each)], dyn, act_t, ctg, inv, wb, wf, wp)
        return c

    lax.fori_loop(0, steps // each, prep, 0)
    step, x = sweep(own, other, dist, duals, init, wb, wf, wp, cx, drive, offs, states, controls)
    lax.fori_loop(0, steps, step, x)
    averaged = [gathered(controls, duals, t) for t in range(robust)]
    put(sums, node_sums(averaged, node_ids(branches[...]), sums.shape[2]))


def second_kernel(scen_total, own, other, dist, duals, init, before, branches, totals, wb, wf, wp, cx,
                  states, controls, sums, averaged_out, drive, offs, linear, duals_now):
    subs, robust, nu, s = duals.shape
    steps = dist.shape[1]
    ids_now = node_ids(branches[...])
    means = node_means(take(totals, subs * nu), robust, scen_total)
    for t in range(robust):
        consensus = spread(means, t, ids_now)
        for i in range(subs):
            c = consensus[i * nu:(i + 1) * nu]
            now = duals[i, t] + before[i, t] - c
            duals_now[i, t] = now
            linear[i, t] = now - c
    step, x = sweep(own, other, dist, linear, init, wb, wf, wp, cx, drive, offs, states, controls)
    lax.fori_loop(0, steps, step, x)
    averaged = []
    for t in range(robust):
        v = gathered(controls, duals_now, t)
        averaged.append(v)
        for i in range(subs):
            averaged_out[i, t] = v[i * nu:(i + 1) * nu]
    put(sums, node_sums(averaged, ids_now, sums.shape[2]))


def last_kernel(scen_total, averaged, branches, totals, out):
    subs, robust, nu, s = averaged.shape
    ids_now = node_ids(branches[...])
    means = node_means(take(totals, subs * nu), robust, scen_total)
    for t in range(robust):
        consensus = spread(means, t, ids_now)
        for i in range(subs):
            out[i, t] = averaged[i, t] - consensus[i * nu:(i + 1) * nu]


def shards(mesh, disturbance, prior_states, initial_state, scaled_duals, dynamics, actuation, cost_to_go,
           inverses, couplers, neighbours, branches):
    subs, steps, nx, s = disturbance.shape
    robust, nu = scaled_duals.shape[1:3]
    ncp = prior_states.shape[2]
    n_scen, n_sub = mesh.shape["scen"], mesh.shape["sub"]
    scen_total = s * n_scen
    swap = [((k + 1) % n_sub, k) for k in range(n_sub)]
    lanes = 2**robust

    vm, sm = pl.BlockSpec(memory_space=pltpu.VMEM), pl.BlockSpec(memory_space=pltpu.SMEM)
    big = jax.ShapeDtypeStruct((subs, steps, nx, s), F32)
    small = jax.ShapeDtypeStruct((subs, steps, nu, s), F32)
    sums = jax.ShapeDtypeStruct((n_scen, -(-subs * nu // n_scen), lanes), F32)
    few = jax.ShapeDtypeStruct((subs, robust, nu, s), F32)
    weights = [
        jax.ShapeDtypeStruct((subs, steps, 2 * nx + nu, 3 * (nx + nu)), BF16),
        jax.ShapeDtypeStruct((subs, steps, nx + nu, 3 * nx), BF16),
        jax.ShapeDtypeStruct((subs, steps, nx, 3 * nx), BF16),
        jax.ShapeDtypeStruct((2, subs * nx, 2 * subs * ncp), BF16),
    ]
    params = pltpu.CompilerParams(vmem_limit_bytes=VMEM_BYTES)
    scratch = [pltpu.VMEM((subs, steps, nx, s), F32), pltpu.VMEM((subs, steps, nu, s), F32)]
    other = lax.ppermute(prior_states, "sub", swap)
    states, controls, partial, *made = pl.pallas_call(
        first_kernel,
        out_shape=[big, small, sums] + weights,
        in_specs=[sm] + [vm] * 11,
        out_specs=[vm] * 7,
        scratch_shapes=scratch,
        compiler_params=params,
    )(neighbours.T, prior_states, other, disturbance, scaled_duals, initial_state, dynamics,
      jnp.swapaxes(actuation, 1, 2), cost_to_go, inverses, couplers, branches)
    other = lax.ppermute(states[:, :, :ncp], "sub", swap)
    totals = all_sum(partial)
    states, controls, partial, averaged = pl.pallas_call(
        functools.partial(second_kernel, scen_total),
        out_shape=[big, small, sums, few],
        in_specs=[vm] * 12,
        out_specs=[vm] * 4,
        scratch_shapes=scratch + [pltpu.VMEM(few.shape, F32), pltpu.VMEM(few.shape, F32)],
        compiler_params=params,
    )(states, other, disturbance, scaled_duals, initial_state, controls[:, :robust], branches, totals, *made)
    totals = all_sum(partial)
    new_duals = pl.pallas_call(
        functools.partial(last_kernel, scen_total),
        out_shape=few,
        in_specs=[vm] * 3,
        out_specs=vm,
        compiler_params=params,
    )(averaged, branches, totals)
    return states, controls, new_duals


def solution(mesh):
    wide_spec = P("sub", None, None, "scen")
    placed = (wide_spec, wide_spec, P("sub", None), wide_spec, P("sub", None, None), P("sub", None, None),
              P("sub", None, None, None), P("sub", None, None, None), P(), P(), P(None, "scen"))
    return jax.shard_map(
        functools.partial(shards, mesh), mesh=mesh, in_specs=placed, out_specs=(wide_spec,) * 3,
        check_vma=False,
    )
```

```python
import functools

import jax
import jax.numpy as jnp
from jax import lax
from jax.experimental import pallas as pl
from jax.experimental.pallas import tpu as pltpu
from jax.sharding import PartitionSpec as P

SWEEPS = 2
F32, BF16 = jnp.float32, jnp.bfloat16
VMEM_BYTES = 56 * 1024 * 1024


def halves(x):
    hi = x.astype(BF16)
    return hi, (x - hi.astype(F32)).astype(BF16)


def wide(w):
    hi, lo = halves(w)
    return jnp.concatenate([hi.astype(F32), lo.astype(F32), hi.astype(F32)], axis=1).astype(BF16)


def tall(x):
    hi, lo = halves(x)
    return jnp.concatenate([hi, hi, lo], axis=0)


def mxu(a, b):
    return jnp.dot(a, b, preferred_element_type=F32)


def dot3(a, b):
    a_hi, a_lo = halves(a)
    b_hi, b_lo = halves(b)
    return mxu(a_hi, b_hi) + (mxu(a_lo, b_hi) + mxu(a_hi, b_lo))


def prepare(times, dyn, act_t, ctg, inv, wb, wf, wp):
    subs, nx = dyn.shape[:2]
    nu = act_t.shape[1]
    work = [(m, t) for t in times for m in range(subs)]
    bt = [act_t[m] for m in range(subs)]
    at = [tall(dyn[m]) for m in range(subs)]
    pa = []
    for m, t in work:
        p = wide(ctg[m, t])
        wp[m, t] = p
        pa.append(mxu(p, at[m]))
    g = [inv[m, t] for m, t in work]
    bg = [dot3(bt[m].T, g[k]) for k, (m, t) in enumerate(work)]
    x2 = [dot3(bt[m], pa[k]) for k, (m, t) in enumerate(work)]
    both = [-jnp.concatenate([g[k], bg[k]], axis=0) for k in range(len(work))]
    low = [dot3(both[k], bt[m]) for k, (m, t) in enumerate(work)]
    gain = [dot3(both[k], x2[k]) for k in range(len(work))]
    for k, (m, t) in enumerate(work):
        front = jnp.concatenate([dyn[m] + gain[k][nu:], gain[k][:nu]], axis=0)
        wf[m, t] = wide(front)
        bottom = jnp.concatenate([low[k], both[k]], axis=1)
        wb[m, t] = wide(jnp.concatenate([front.T, bottom], axis=0))


def stepped(count, step, carry, each=4):
    def several(k, c):
        for r in range(each):
            c = step(k * each + r, c)
        return c

    carry = lax.fori_loop(0, count // each, several, carry)
    return lax.fori_loop(count // each * each, count, step, carry)


def couple(subs, own_first, other_first, neigh, coup, cx):
    nb, nx, ncp = coup.shape[1:]
    for side, first in enumerate((own_first, other_first)):
        for i in range(subs):
            for j in range(subs):
                total = jnp.zeros((nx, ncp), F32)
                for e in range(nb):
                    hit = neigh[e, own_first + i] == first + j
                    total = total + jnp.where(hit, coup[own_first + i, e], 0.0)
                hi, lo = halves(total)
                at = (side * subs + j) * ncp
                cx[0, i * nx:(i + 1) * nx, at:at + ncp] = hi
                cx[1, i * nx:(i + 1) * nx, at:at + ncp] = lo


def influence(t, own, other, cx):
    subs = own.shape[0]
    blocks = [own[j, t] for j in range(subs)] + [other[j, t] for j in range(subs)]
    x = jnp.concatenate(blocks, axis=0)
    hi, lo = halves(x)
    return mxu(cx[0], hi) + mxu(cx[1], hi) + mxu(cx[0], lo)


def sweep(own, other, dist, linear, init, wb, wf, wp, cx, drive, offs, states, controls):
    subs, steps, nx, s = dist.shape
    nu = controls.shape[2]
    robust = linear.shape[1]

    def grow(t):
        flow = influence(t, own, other, cx)
        out = []
        for i in range(subs):
            d = dist[i, t] + flow[i * nx:(i + 1) * nx]
            drive[i, t] = d
            out.append(mxu(wp[i, t], tall(d)))
        return tuple(out)

    def back(t, carry, with_linear):
        costate, q = carry
        ahead = grow(jnp.maximum(t - 1, 0))
        after = []
        for i in range(subs):
            push = linear[i, t] if with_linear else jnp.zeros((nu, s), F32)
            y = mxu(wb[i, t], tall(jnp.concatenate([q[i] + costate[i], push], axis=0)))
            offs[i, t] = y[nx:nx + nu]
            states[i, t] = y[nx + nu:]
            after.append(y[:nx])
        return tuple(after), ahead

    zero = tuple(jnp.zeros((nx, s), F32) for _ in range(subs))
    carry = (zero, grow(steps - 1))
    carry = stepped(steps - robust, lambda k, c: back(steps - 1 - k, c, False), carry)
    carry = lax.fori_loop(0, robust, lambda k, c: back(robust - 1 - k, c, True), carry)

    def ahead(t, x):
        after = []
        for i in range(subs):
            y = mxu(wf[i, t], tall(x[i]))
            controls[i, t] = y[nx:] + offs[i, t]
            now = y[:nx] + (states[i, t] + drive[i, t])
            states[i, t] = now
            after.append(now)
        return tuple(after)

    x = tuple(jnp.broadcast_to(init[...].T[:, i:i + 1], (nx, s)) for i in range(subs))
    return ahead, x


def member(t, ids, lanes):
    s = ids.shape[1]
    place = lax.broadcasted_iota(jnp.int32, (lanes, s), 0)
    return jnp.where(place == ids[t:t + 1, :] + (2**t - 1), 1.0, 0.0).astype(BF16)


def node_ids(branches):
    rows = [jnp.zeros((1, branches.shape[1]), jnp.int32)]
    for k in range(branches.shape[0]):
        rows.append(rows[-1] + branches[k:k + 1] * 2**k)
    return jnp.concatenate(rows, axis=0)


def put(sums, values):
    count, rows, lanes = sums.shape
    extra = count * rows - values.shape[0]
    if extra:
        values = jnp.concatenate([values, jnp.zeros((extra, lanes), F32)], axis=0)
    for k in range(count):
        sums[k] = values[k * rows:(k + 1) * rows]


def take(totals, rows):
    return jnp.concatenate([totals[k] for k in range(-(-rows // totals.shape[1]))], axis=0)[:rows]


def reduce_kernel(part, out, land, full, send_a, recv_a, send_b, recv_b):
    n = part.shape[0]
    me = lax.axis_index("scen")
    barrier = pltpu.get_barrier_semaphore()

    def over(step):
        def body(k, c):
            step(k, lax.rem(me + k, n))
            return c

        lax.fori_loop(1, n, body, 0)

    def piece(k, to):
        return pltpu.make_async_remote_copy(
            src_ref=part.at[to], dst_ref=land.at[k], send_sem=send_a.at[k], recv_sem=recv_a.at[k],
            device_id={"scen": to}, device_id_type=pl.DeviceIdType.MESH)

    def whole(k, to):
        return pltpu.make_async_remote_copy(
            src_ref=full.at[me], dst_ref=full.at[me], send_sem=send_b.at[k], recv_sem=recv_b.at[k],
            device_id={"scen": to}, device_id_type=pl.DeviceIdType.MESH)

    over(lambda k, to: pl.semaphore_signal(
        barrier, inc=1, device_id={"scen": to}, device_id_type=pl.DeviceIdType.MESH))
    pl.semaphore_wait(barrier, n - 1)
    over(lambda k, to: piece(k, to).start())
    over(lambda k, to: piece(k, to).wait_recv())
    full[me] = lax.fori_loop(1, n, lambda k, c: c + land[k], part[me])
    over(lambda k, to: whole(k, to).start())
    over(lambda k, to: piece(k, to).wait_send())
    over(lambda k, to: whole(k, to).wait_recv())
    over(lambda k, to: whole(k, to).wait_send())
    out[...] = full[...]


def all_sum(part):
    n = part.shape[0]
    vm = pl.BlockSpec(memory_space=pltpu.VMEM)
    return pl.pallas_call(
        reduce_kernel,
        out_shape=jax.ShapeDtypeStruct(part.shape, F32),
        in_specs=[vm],
        out_specs=vm,
        scratch_shapes=[pltpu.VMEM(part.shape, F32)] * 2 + [pltpu.SemaphoreType.DMA((n,))] * 4,
        compiler_params=pltpu.CompilerParams(collective_id=0, has_side_effects=True),
    )(part)


def node_sums(averaged, ids, lanes):
    robust = len(averaged)
    total = None
    for t in range(robust):
        hot = member(t, ids, lanes)
        for part in halves(averaged[t]):
            term = lax.dot_general(part, hot, (((1,), (1,)), ((), ())), preferred_element_type=F32)
            total = term if total is None else total + term
    return total


def node_means(totals, robust, scen_total):
    place = lax.broadcasted_iota(jnp.int32, totals.shape, 1)
    shares = jnp.ones(totals.shape, F32)
    for t in range(1, robust):
        shares = jnp.where(place >= 2**t - 1, float(2**t), shares)
    return totals * (shares / float(scen_total))


def spread(means, t, ids):
    hot = member(t, ids, means.shape[1])
    hi, lo = halves(means)
    return mxu(hi, hot) + mxu(lo, hot)


def gathered(controls, duals, t):
    subs = duals.shape[0]
    return jnp.concatenate([controls[i, t] + duals[i, t] for i in range(subs)], axis=0)


def first_kernel(neigh, own, other, dist, duals, init, dyn, act_t, ctg, inv, coup, branches,
                 states, controls, sums, wb, wf, wp, cx, drive, offs):
    subs, robust = duals.shape[:2]
    steps = dist.shape[1]
    n_sub = coup.shape[0] // subs
    me = lax.axis_index("sub")
    couple(subs, me * subs, lax.rem(me + 1, n_sub) * subs, neigh, coup, cx)
    each = 4 if steps % 4 == 0 else 1

    def prep(k, c):
        prepare([k * each + r for r in range(each)], dyn, act_t, ctg, inv, wb, wf, wp)
        return c

    lax.fori_loop(0, steps // each, prep, 0)
    step, x = sweep(own, other, dist, duals, init, wb, wf, wp, cx, drive, offs, states, controls)
    stepped(steps, step, x)
    averaged = [gathered(controls, duals, t) for t in range(robust)]
    put(sums, node_sums(averaged, node_ids(branches[...]), sums.shape[2]))


def second_kernel(scen_total, own, other, dist, duals, init, before, branches, totals, wb, wf, wp, cx,
                  states, controls, sums, averaged_out, drive, offs, linear, duals_now):
    subs, robust, nu, s = duals.shape
    steps = dist.shape[1]
    ids_now = node_ids(branches[...])
    means = node_means(take(totals, subs * nu), robust, scen_total)
    for t in range(robust):
        consensus = spread(means, t, ids_now)
        for i in range(subs):
            c = consensus[i * nu:(i + 1) * nu]
            now = duals[i, t] + before[i, t] - c
            duals_now[i, t] = now
            linear[i, t] = now - c
    step, x = sweep(own, other, dist, linear, init, wb, wf, wp, cx, drive, offs, states, controls)
    stepped(steps, step, x)
    averaged = []
    for t in range(robust):
        v = gathered(controls, duals_now, t)
        averaged.append(v)
        for i in range(subs):
            averaged_out[i, t] = v[i * nu:(i + 1) * nu]
    put(sums, node_sums(averaged, ids_now, sums.shape[2]))


def last_kernel(scen_total, averaged, branches, totals, out):
    subs, robust, nu, s = averaged.shape
    ids_now = node_ids(branches[...])
    means = node_means(take(totals, subs * nu), robust, scen_total)
    for t in range(robust):
        consensus = spread(means, t, ids_now)
        for i in range(subs):
            out[i, t] = averaged[i, t] - consensus[i * nu:(i + 1) * nu]


def shards(mesh, disturbance, prior_states, initial_state, scaled_duals, dynamics, actuation, cost_to_go,
           inverses, couplers, neighbours, branches):
    subs, steps, nx, s = disturbance.shape
    robust, nu = scaled_duals.shape[1:3]
    ncp = prior_states.shape[2]
    n_scen, n_sub = mesh.shape["scen"], mesh.shape["sub"]
    scen_total = s * n_scen
    swap = [((k + 1) % n_sub, k) for k in range(n_sub)]
    lanes = 2**robust

    vm, sm = pl.BlockSpec(memory_space=pltpu.VMEM), pl.BlockSpec(memory_space=pltpu.SMEM)
    big = jax.ShapeDtypeStruct((subs, steps, nx, s), F32)
    small = jax.ShapeDtypeStruct((subs, steps, nu, s), F32)
    sums = jax.ShapeDtypeStruct((n_scen, -(-subs * nu // n_scen), lanes), F32)
    few = jax.ShapeDtypeStruct((subs, robust, nu, s), F32)
    weights = [
        jax.ShapeDtypeStruct((subs, steps, 2 * nx + nu, 3 * (nx + nu)), BF16),
        jax.ShapeDtypeStruct((subs, steps, nx + nu, 3 * nx), BF16),
        jax.ShapeDtypeStruct((subs, steps, nx, 3 * nx), BF16),
        jax.ShapeDtypeStruct((2, subs * nx, 2 * subs * ncp), BF16),
    ]
    params = pltpu.CompilerParams(vmem_limit_bytes=VMEM_BYTES)
    scratch = [pltpu.VMEM((subs, steps, nx, s), F32), pltpu.VMEM((subs, steps, nu, s), F32)]
    other = lax.ppermute(prior_states, "sub", swap)
    states, controls, partial, *made = pl.pallas_call(
        first_kernel,
        out_shape=[big, small, sums] + weights,
        in_specs=[sm] + [vm] * 11,
        out_specs=[vm] * 7,
        scratch_shapes=scratch,
        compiler_params=params,
    )(neighbours.T, prior_states, other, disturbance, scaled_duals, initial_state, dynamics,
      jnp.swapaxes(actuation, 1, 2), cost_to_go, inverses, couplers, branches)
    other = lax.ppermute(states[:, :, :ncp], "sub", swap)
    totals = all_sum(partial)
    states, controls, partial, averaged = pl.pallas_call(
        functools.partial(second_kernel, scen_total),
        out_shape=[big, small, sums, few],
        in_specs=[vm] * 12,
        out_specs=[vm] * 4,
        scratch_shapes=scratch + [pltpu.VMEM(few.shape, F32), pltpu.VMEM(few.shape, F32)],
        compiler_params=params,
    )(states, other, disturbance, scaled_duals, initial_state, controls[:, :robust], branches, totals, *made)
    totals = all_sum(partial)
    new_duals = pl.pallas_call(
        functools.partial(last_kernel, scen_total),
        out_shape=few,
        in_specs=[vm] * 3,
        out_specs=vm,
        compiler_params=params,
    )(averaged, branches, totals)
    return states, controls, new_duals


def solution(mesh):
    wide_spec = P("sub", None, None, "scen")
    placed = (wide_spec, wide_spec, P("sub", None), wide_spec, P("sub", None, None), P("sub", None, None),
              P("sub", None, None, None), P("sub", None, None, None), P(), P(), P(None, "scen"))
    return jax.shard_map(
        functools.partial(shards, mesh), mesh=mesh, in_specs=placed, out_specs=(wide_spec,) * 3,
        check_vma=False,
    )
```
